32 devices in a mesh: grp: 2 (over x), dp: 4 (over y, core), mp: 4 (over z).
Axes of the slice: x: 2, y: 2, z: 4, core: 2. Of those that a mesh axis runs over, the one named last changes fastest.
Arguments:
- queries: bfloat16 [4, 512, 4096], P('dp', None, 'mp'), may hold values from -5 to 5
- keys: bfloat16 [4, 512, 512], P('dp'), may hold values from -5 to 5
- values: bfloat16 [4, 512, 512], P('dp'), may hold values from -6 to 6
- out_weight: bfloat16 [4096, 5120], P('mp'), may hold values from -0.09375 to 0.09375
- residual: bfloat16 [4, 512, 5120], P('dp', 'mp'), may hold values from -24 to 24
- student_hidden: bfloat16 [4, 512, 2560], P('dp', 'mp'), may hold values from -6 to 6
- norm_gain: float32 [2560], replicated, may hold values from 0.5 to 1.5
- projection: bfloat16 [2560, 5120], P(None, ('grp', 'dp')), may hold values from -0.125 to 0.125
- lengths: int32 [4], replicated, may hold values from 128 to 512, as said below
Outputs:
- teacher_out: bfloat16 [4, 512, 5120], P('dp', 'mp', 'grp')
- distill_loss: float32 [], replicated
- grad_proj: float32 [2560, 5120], P('mp', ('grp', 'dp'))
- grad_gain: float32 [2560], P('grp')
- grad_hidden: float32 [4, 512, 2560], P('dp', 'mp', 'grp')
The draws below stay inside these ranges and needn't reach their ends.
Inputs may be any that keep to these rules, and one draw needn't show every extreme that they name: `lengths`: at least one sequence is live throughout.
All inputs are finite; a program needn't handle non-finite values.
Results may differ from the reference program's by a relative error of at most 0.018.
Values may be sent and summed in bfloat16 or wider, within the bound.
A program may use at most 128 MiB of HBM per device.

```python
import jax
import jax.numpy as jnp
from jax import lax

D_T = 5120
D_S = 2560
HD = 128
HQ = 32
KVH = 4
L = 512
SEQS = 4
N_MP = 4


def draw_keys(key, part):
    key = jax.random.fold_in(key, 7)
    sampled = jax.random.truncated_normal(key, -5.0, 5.0, (SEQS, L, KVH * HD), jnp.float32)
    return sampled.astype(jnp.bfloat16)


def draw_queries(key, part):
    key = jax.random.fold_in(key, 9)
    sampled = jax.random.truncated_normal(key, -5.0, 5.0, (SEQS, L, HQ * HD), jnp.float32)
    return sampled.astype(jnp.bfloat16)


def column_scales(low, high):
    ramp = jnp.arange(D_T, dtype=jnp.float32) / (D_T - 1)
    return jnp.exp(jnp.log(low) + ramp * (jnp.log(high) - jnp.log(low)))


def draw_residual(key, part):
    key = jax.random.fold_in(key, 11)
    sampled = jax.random.truncated_normal(key, -6.0, 6.0, (SEQS, L, D_T), jnp.float32)
    scales = column_scales(0.5, 3.0)
    return (sampled * scales[None, None, :]).astype(jnp.bfloat16)


def draw_lengths(key, part):
    key = jax.random.fold_in(key, 5)
    first_key, second_key = jax.random.split(key)
    sampled = jax.random.randint(first_key, (SEQS,), L // 4, L + 1)
    full_index = jax.random.randint(second_key, (), 0, SEQS)
    return jnp.where(jnp.arange(SEQS) == full_index, L, sampled).astype(jnp.int32)


def shard_levels(key, extent, shards, low, high):
    loudness = 1.0
    for dim, shards_of in shards:
        steps = jax.random.uniform(jax.random.fold_in(jax.random.fold_in(key, 6), dim), (shards_of,), jnp.float32, low / len(shards), high / len(shards))
        loudness = loudness * jnp.repeat(jnp.exp(steps), extent[dim] // shards_of).reshape((-1,) + (1,) * (len(extent) - 1 - dim))
    return loudness


def noise(rng, dims, width, most, shards=(), held_as=jnp.bfloat16):
    level = shard_levels(rng, dims, shards, -0.22, 0.18) if shards else 1.0
    entries = jax.random.normal(rng, dims, jnp.float32) * width * level
    return jnp.minimum(jnp.maximum(entries, -most), most).astype(held_as)


def setup_inputs(seed: int = 0) -> dict:
    key_of = jax.random.split(jax.random.key(seed), 10)
    queries = draw_queries(jax.random.fold_in(key_of[9], 71), 0)
    keys = draw_keys(jax.random.fold_in(key_of[9], 71), 0)
    values = noise(key_of[2], (SEQS, L, KVH * HD), 1.0, 6.0, ((0, 4),))
    out_weight = noise(key_of[3], (HQ * HD, D_T), (HQ * HD) ** -0.5, 0.09375, ((0, 4),))
    residual = draw_residual(jax.random.fold_in(key_of[9], 71), 0)
    student_hidden = noise(key_of[5], (SEQS, L, D_S), 1.0, 6.0, ((0, 4), (1, 4)))
    norm_gain = jnp.clip(1.0 + 0.1 * jax.random.normal(key_of[6], (D_S,), jnp.float32), 0.5, 1.5)
    projection = noise(key_of[7], (D_S, D_T), D_S ** -0.5, 0.125, ((1, 8),))
    lengths = draw_lengths(jax.random.fold_in(key_of[9], 71), 0)
    return dict(queries=queries, keys=keys, values=values, out_weight=out_weight, residual=residual, student_hidden=student_hidden, norm_gain=norm_gain, projection=projection, lengths=lengths)


def attend_heads(query_heads, key_heads, value_heads):
    seq_len = query_heads.shape[0]
    positions = jnp.arange(seq_len, dtype=jnp.int32)
    scores = jnp.einsum('qgd,kgd->gqk', query_heads.astype(jnp.float32), key_heads.astype(jnp.float32)) * HD ** (-0.5)
    allowed = positions[None, :, None] >= positions[None, None, :]
    scores = jnp.where(allowed, scores, -1e+30)
    row_max = lax.optimization_barrier(jnp.max(scores, axis=-1, keepdims=True))
    exponent = jnp.exp(scores - row_max)
    weights = (exponent / lax.optimization_barrier(jnp.sum(exponent, axis=-1, keepdims=True))).astype(jnp.bfloat16)
    context = jnp.einsum('gqk,kgd->qgd', weights.astype(jnp.float32), value_heads.astype(jnp.float32))
    return context.reshape(seq_len, -1).astype(jnp.bfloat16)

def teacher_rows(query_seq, key_seq, value_seq, out_weight, residual_seq):
    seq_len = query_seq.shape[0]
    group_heads = HQ // N_MP
    shared = HQ // KVH
    query_groups = query_seq.reshape(seq_len, N_MP, group_heads, HD).transpose(1, 0, 2, 3)
    weight_groups = out_weight.reshape(N_MP, group_heads * HD, D_T)
    key_heads = key_seq.reshape(seq_len, KVH, HD)
    value_heads = value_seq.reshape(seq_len, KVH, HD)

    def add_group(summed, inputs):
        query_group, weight_group, group_index = inputs
        kv_index = ((group_index * group_heads + jnp.arange(group_heads, dtype=jnp.int32)) // shared).astype(jnp.int32)
        context = attend_heads(query_group, jnp.take(key_heads, kv_index, axis=1), jnp.take(value_heads, kv_index, axis=1))
        partial_sum = jnp.dot(context, weight_group, preferred_element_type=jnp.float32).astype(jnp.bfloat16)
        partial_sum = lax.optimization_barrier(partial_sum)
        return (summed + partial_sum.astype(jnp.float32), None)
    summed, unused = lax.scan(add_group, jnp.zeros((seq_len, D_T), jnp.float32), (query_groups, weight_groups, jnp.arange(N_MP, dtype=jnp.int32)))
    return (residual_seq.astype(jnp.float32) + summed).astype(jnp.bfloat16)

def reference(queries, keys, values, out_weight, residual, student_hidden, norm_gain, projection, lengths):
    teacher_out = jnp.stack([teacher_rows(queries[sequence], keys[sequence], values[sequence], out_weight, residual[sequence]) for sequence in range(SEQS)])
    hidden = student_hidden.reshape(-1, D_S).astype(jnp.float32)
    inverse_rms = lax.rsqrt(lax.optimization_barrier(jnp.mean(hidden * hidden, axis=-1, keepdims=True)) + 1e-06)
    unit = hidden * inverse_rms
    normed = (unit * norm_gain).astype(jnp.bfloat16)
    predicted = jnp.dot(normed, projection, preferred_element_type=jnp.float32)
    positions = jnp.arange(L, dtype=jnp.int32)
    live_rows = (positions[None, :] < lengths[:, None]).reshape(-1, 1)
    live_count = jnp.sum(lengths).astype(jnp.float32)
    difference = jnp.where(live_rows, predicted - teacher_out.reshape(-1, D_T).astype(jnp.float32), 0.0)
    distill_loss = jnp.sum(difference * difference) / (live_count * D_T)
    grad_pred = difference.astype(jnp.bfloat16)
    grad_proj = lax.dot_general(normed, grad_pred, (((0,), (0,)), ((), ())), preferred_element_type=jnp.float32) / live_count
    grad_normed = lax.dot_general(grad_pred, projection, (((1,), (1,)), ((), ())), preferred_element_type=jnp.float32)
    grad_gain = lax.optimization_barrier(jnp.sum(grad_normed * unit, axis=0)) / live_count
    scaled = grad_normed * norm_gain
    mean_term = lax.optimization_barrier(jnp.sum(scaled * unit, axis=-1, keepdims=True)) / D_S
    grad_hidden = inverse_rms * (scaled - unit * mean_term)
    return (teacher_out, distill_loss, grad_proj, grad_gain, grad_hidden.reshape(SEQS, L, D_S))
```

```python
import jax
import jax.numpy as jnp
from jax import lax
from jax.experimental import pallas as pl
from jax.experimental.pallas import tpu as pltpu
from jax.sharding import PartitionSpec as P

D_T = 5120
D_S = 2560
HD = 128
HQ = 32
KVH = 4
BF = jnp.bfloat16
F32 = jnp.float32


def swap(array, axis, flip):
    return lax.ppermute(array, axis, [(i, i ^ flip) for i in range(lax.axis_size(axis))])


def attend_kernel(q_ref, k_ref, v_ref, o_ref):
    rows, keys = q_ref.shape[0], k_ref.shape[0]
    scores = lax.dot_general(
        q_ref[...], k_ref[...], (((1,), (1,)), ((), ())), preferred_element_type=F32
    ) * (HD ** (-0.5))
    row_ids = pl.program_id(1) * rows + lax.broadcasted_iota(jnp.int32, (rows, keys), 0)
    key_ids = lax.broadcasted_iota(jnp.int32, (rows, keys), 1)
    scores = jnp.where(row_ids >= key_ids, scores, -1e30)
    exponent = jnp.exp(scores - jnp.max(scores, axis=-1, keepdims=True))
    total = jnp.sum(exponent, axis=-1, keepdims=True)
    weights = (exponent * (1.0 / total)).astype(BF)
    o_ref[...] = jnp.dot(weights, v_ref[...], preferred_element_type=F32).astype(BF)


def attend(queries, key_rows, value_rows):
    rows, width = queries.shape
    block = min(256, rows)
    keys = key_rows.shape[0]
    whole = pl.BlockSpec((keys, HD), lambda h, b: (0, 0))
    tile = pl.BlockSpec((block, HD), lambda h, b: (b, h))
    return pl.pallas_call(
        attend_kernel,
        grid=(width // HD, rows // block),
        in_specs=[tile, whole, whole],
        out_specs=tile,
        out_shape=jax.ShapeDtypeStruct((rows, width), BF),
        compiler_params=pltpu.CompilerParams(vmem_limit_bytes=32 * 1024 * 1024),
        cost_estimate=pl.CostEstimate(
            flops=4 * rows * keys * width,
            bytes_accessed=4 * rows * width + 4 * keys * HD,
            transcendentals=rows * keys * (width // HD),
        ),
    )(queries, key_rows, value_rows)


def line_scatter_sum(parts, axis, subs):
    n = lax.axis_size(axis)
    me = lax.axis_index(axis)
    rows = parts.shape[0] // n
    cols = parts.shape[1] // subs

    def term(block, sub):
        start = lax.rem(block + n, n) * rows
        return lax.dynamic_slice(parts, (start, sub * cols), (rows, cols))

    ups, downs = [None] * subs, [None] * subs
    for t in range(1, n):
        up_pairs = [(i, i + 1) for i in range(t)]
        down_pairs = [(n - 1 - i, n - 2 - i) for i in range(t)]
        for sub in range(subs):
            up, down = term(me + n - t, sub), term(me + t - n, sub)
            if t > 1:
                up = (up.astype(F32) + ups[sub].astype(F32)).astype(BF)
                down = (down.astype(F32) + downs[sub].astype(F32)).astype(BF)
            ups[sub] = lax.ppermute(up, axis, up_pairs)
            downs[sub] = lax.ppermute(down, axis, down_pairs)
    sums = [
        term(me, sub).astype(F32) + ups[sub].astype(F32) + downs[sub].astype(F32)
        for sub in range(subs)
    ]
    return jnp.concatenate(sums, axis=1)


def body(
    queries, keys, values, out_weight, residual, student_hidden, norm_gain, projection, lengths
):
    tok_rows = residual.shape[1]
    half_cols = residual.shape[2] // 2
    width_half = norm_gain.shape[0] // 2
    shard_cols = projection.shape[1]
    grp = lax.axis_index("grp")
    dp = lax.axis_index("dp")
    mp = lax.axis_index("mp")
    dp_hi, dp_lo = dp // 2, dp % 2

    hidden = student_hidden[0].astype(F32)
    inverse_rms = lax.rsqrt(jnp.mean(hidden * hidden, axis=-1, keepdims=True) + 1e-06)
    normed = (hidden * inverse_rms * norm_gain).astype(BF)
    normed_pair = jnp.concatenate([normed, swap(normed, "dp", 2)], axis=0)
    normed_all = jnp.concatenate([normed_pair, swap(normed_pair, "dp", 1)], axis=0)

    local_heads = queries.shape[2] // HD
    kv_head = mp * local_heads // (HQ // KVH)
    key_rows = lax.dynamic_slice_in_dim(keys[0], kv_head * HD, HD, 1)
    value_rows = lax.dynamic_slice_in_dim(values[0], kv_head * HD, HD, 1)
    context = attend(queries[0], key_rows, value_rows)
    weight_half = lax.dynamic_slice_in_dim(out_weight, grp * half_cols, half_cols, 1)
    attn_part = jnp.dot(context, weight_half, preferred_element_type=F32).astype(BF)
    attn_rows = line_scatter_sum(attn_part, "mp", 2)
    residual_half = lax.dynamic_slice_in_dim(residual[0], grp * half_cols, half_cols, 1)
    own_target = (residual_half.astype(F32) + attn_rows).astype(BF)

    pair_cols = 2 * shard_cols
    kept = lax.dynamic_slice_in_dim(own_target, dp_hi * pair_cols, pair_cols, 1)
    sent = lax.dynamic_slice_in_dim(own_target, (1 - dp_hi) * pair_cols, pair_cols, 1)
    target_pair = jnp.concatenate([kept, swap(sent, "dp", 2)], axis=0)
    kept = lax.dynamic_slice_in_dim(target_pair, dp_lo * shard_cols, shard_cols, 1)
    sent = lax.dynamic_slice_in_dim(target_pair, (1 - dp_lo) * shard_cols, shard_cols, 1)
    targets = jnp.concatenate([kept, swap(sent, "dp", 1)], axis=0)

    predicted = jnp.dot(normed_all, projection, preferred_element_type=F32)
    position = mp * tok_rows + jnp.arange(tok_rows, dtype=jnp.int32)
    live_rows = jnp.concatenate([position < lengths[dp ^ flip] for flip in (0, 2, 1, 3)])
    difference = jnp.where(live_rows[:, None], predicted - targets.astype(F32), 0.0)
    live_count = jnp.sum(lengths).astype(F32)
    squared = jnp.sum(difference * difference)
    grad_pred = difference.astype(BF)

    def pull_back(rows):
        return lax.dot_general(
            rows, projection, (((1,), (1,)), ((), ())), preferred_element_type=F32
        )

    arrived = swap(pull_back(grad_pred[2 * tok_rows :]).astype(BF), "dp", 1)
    pulled = pull_back(grad_pred[: 2 * tok_rows]) + arrived.astype(F32)
    pulled = pulled.reshape(2, tok_rows, 2 * width_half)
    half_rows = tok_rows // 2

    def own_half(array):
        return lax.dynamic_slice_in_dim(array, grp * width_half, width_half, array.ndim - 1)

    def other_half(array):
        return lax.dynamic_slice_in_dim(array, (1 - grp) * width_half, width_half, array.ndim - 1)

    first = pulled[:, :half_rows]
    second = pulled[:, half_rows:]
    first_in = swap(first[1].astype(BF), "dp", 2)
    second_in = swap(other_half(second).astype(BF), "grp", 1)
    first = first[0] + first_in.astype(F32)
    second = own_half(second) + second_in.astype(F32)
    first_in = swap(other_half(first).astype(BF), "grp", 1)
    second_in = swap(second[1].astype(BF), "dp", 2)
    grad_half = jnp.concatenate(
        [own_half(first) + first_in.astype(F32), second[0] + second_in.astype(F32)], axis=0
    )

    grad_proj_part = lax.dot_general(
        normed_all, grad_pred, (((0,), (0,)), ((), ())), preferred_element_type=F32
    ).astype(BF)
    grad_proj = line_scatter_sum(grad_proj_part, "mp", 1) / live_count

    gain_half = own_half(norm_gain)
    unit_half = own_half(hidden) * inverse_rms
    scaled = grad_half * gain_half
    inner_sum = jnp.sum(scaled * unit_half, axis=-1)
    inner_sum = inner_sum + swap(inner_sum, "grp", 1)
    mean_term = inner_sum[:, None] / D_S
    grad_hidden = inverse_rms * (scaled - unit_half * mean_term)

    sums = jnp.concatenate(
        [jnp.sum(grad_half * unit_half, axis=0), jnp.full((128,), squared, F32)]
    )
    gathered = lax.all_gather(sums, ("grp", "dp", "mp"), axis=0, tiled=False)
    gathered = gathered.reshape(lax.axis_size("grp"), -1, width_half + 128)
    grad_gain = (
        jnp.sum(lax.dynamic_index_in_dim(gathered, grp, 0, False)[:, :width_half], axis=0)
        / live_count
    )
    distill_loss = jnp.sum(gathered[:, :, width_half]) / (live_count * D_T)
    return (own_target[None], distill_loss, grad_proj, grad_gain, grad_hidden[None])


def solution(mesh):
    in_specs = (
        P("dp", None, "mp"),
        P("dp", None, None),
        P("dp", None, None),
        P("mp", None),
        P("dp", "mp", None),
        P("dp", "mp", None),
        P(),
        P(None, ("grp", "dp")),
        P(),
    )
    out_specs = (P("dp", "mp", "grp"), P(), P("mp", ("grp", "dp")), P("grp"), P("dp", "mp", "grp"))
    return jax.shard_map(body, mesh=mesh, in_specs=in_specs, out_specs=out_specs, check_vma=False)
```

```python
import jax
import jax.numpy as jnp
from jax import lax
from jax.experimental import pallas as pl
from jax.experimental.pallas import tpu as pltpu
from jax.sharding import PartitionSpec as P

D_T = 5120
D_S = 2560
HD = 128
HQ = 32
KVH = 4
BF = jnp.bfloat16
F32 = jnp.float32


def swap(array, axis, flip):
    return lax.ppermute(array, axis, [(i, i ^ flip) for i in range(lax.axis_size(axis))])


def attend_kernel(q_ref, k_ref, v_ref, o_ref):
    rows, keys = q_ref.shape[0], k_ref.shape[0]
    scores = lax.dot_general(
        q_ref[...], k_ref[...], (((1,), (1,)), ((), ())), preferred_element_type=F32
    ) * (HD ** (-0.5))
    row_ids = pl.program_id(1) * rows + lax.broadcasted_iota(jnp.int32, (rows, keys), 0)
    key_ids = lax.broadcasted_iota(jnp.int32, (rows, keys), 1)
    scores = jnp.where(row_ids >= key_ids, scores, -1e30)
    exponent = jnp.exp(scores - jnp.max(scores, axis=-1, keepdims=True))
    total = jnp.sum(exponent, axis=-1, keepdims=True)
    weights = (exponent * (1.0 / total)).astype(BF)
    o_ref[...] = jnp.dot(weights, v_ref[...], preferred_element_type=F32).astype(BF)


def attend(queries, key_rows, value_rows):
    rows, width = queries.shape
    block = min(256, rows)
    keys = key_rows.shape[0]
    whole = pl.BlockSpec((keys, HD), lambda h, b: (0, 0))
    tile = pl.BlockSpec((block, HD), lambda h, b: (b, h))
    return pl.pallas_call(
        attend_kernel,
        grid=(width // HD, rows // block),
        in_specs=[tile, whole, whole],
        out_specs=tile,
        out_shape=jax.ShapeDtypeStruct((rows, width), BF),
        compiler_params=pltpu.CompilerParams(vmem_limit_bytes=32 * 1024 * 1024),
        cost_estimate=pl.CostEstimate(
            flops=4 * rows * keys * width,
            bytes_accessed=4 * rows * width + 4 * keys * HD,
            transcendentals=rows * keys * (width // HD),
        ),
    )(queries, key_rows, value_rows)


def line_scatter_sum(parts, axis, subs):
    n = lax.axis_size(axis)
    me = lax.axis_index(axis)
    rows = parts.shape[0] // n
    cols = parts.shape[1] // subs

    def term(block, sub):
        start = lax.rem(block + n, n) * rows
        return lax.dynamic_slice(parts, (start, sub * cols), (rows, cols))

    ups, downs = [None] * subs, [None] * subs
    for t in range(1, n):
        up_pairs = [(i, i + 1) for i in range(t)]
        down_pairs = [(n - 1 - i, n - 2 - i) for i in range(t)]
        for sub in range(subs):
            up, down = term(me + n - t, sub), term(me + t - n, sub)
            if t > 1:
                up = (up.astype(F32) + ups[sub].astype(F32)).astype(BF)
                down = (down.astype(F32) + downs[sub].astype(F32)).astype(BF)
            ups[sub] = lax.ppermute(up, axis, up_pairs)
            downs[sub] = lax.ppermute(down, axis, down_pairs)
    sums = [
        term(me, sub).astype(F32) + ups[sub].astype(F32) + downs[sub].astype(F32)
        for sub in range(subs)
    ]
    return jnp.concatenate(sums, axis=1)


def body(
    queries, keys, values, out_weight, residual, student_hidden, norm_gain, projection, lengths
):
    tok_rows = residual.shape[1]
    half_cols = residual.shape[2] // 2
    width_half = norm_gain.shape[0] // 2
    shard_cols = projection.shape[1]
    grp = lax.axis_index("grp")
    dp = lax.axis_index("dp")
    mp = lax.axis_index("mp")
    dp_hi, dp_lo = dp // 2, dp % 2

    hidden = student_hidden[0].astype(F32)
    inverse_rms = lax.rsqrt(jnp.mean(hidden * hidden, axis=-1, keepdims=True) + 1e-06)
    normed = (hidden * inverse_rms * norm_gain).astype(BF)
    normed_pair = jnp.concatenate([normed, swap(normed, "dp", 2)], axis=0)
    normed_all = jnp.concatenate([normed_pair, swap(normed_pair, "dp", 1)], axis=0)

    local_heads = queries.shape[2] // HD
    kv_head = mp * local_heads // (HQ // KVH)
    key_rows = lax.dynamic_slice_in_dim(keys[0], kv_head * HD, HD, 1)
    value_rows = lax.dynamic_slice_in_dim(values[0], kv_head * HD, HD, 1)
    context = attend(queries[0], key_rows, value_rows)
    weight_half = lax.dynamic_slice_in_dim(out_weight, grp * half_cols, half_cols, 1)
    attn_part = jnp.dot(context, weight_half, preferred_element_type=F32).astype(BF)
    attn_rows = line_scatter_sum(attn_part, "mp", 2)
    residual_half = lax.dynamic_slice_in_dim(residual[0], grp * half_cols, half_cols, 1)
    own_target = (residual_half.astype(F32) + attn_rows).astype(BF)

    pair_cols = 2 * shard_cols
    kept = lax.dynamic_slice_in_dim(own_target, dp_hi * pair_cols, pair_cols, 1)
    sent = lax.dynamic_slice_in_dim(own_target, (1 - dp_hi) * pair_cols, pair_cols, 1)
    target_pair = jnp.concatenate([kept, swap(sent, "dp", 2)], axis=0)
    kept = lax.dynamic_slice_in_dim(target_pair, dp_lo * shard_cols, shard_cols, 1)
    sent = lax.dynamic_slice_in_dim(target_pair, (1 - dp_lo) * shard_cols, shard_cols, 1)
    targets = jnp.concatenate([kept, swap(sent, "dp", 1)], axis=0)

    predicted = jnp.dot(normed_all, projection, preferred_element_type=F32)
    position = mp * tok_rows + jnp.arange(tok_rows, dtype=jnp.int32)
    live_rows = jnp.concatenate([position < lengths[dp ^ flip] for flip in (0, 2, 1, 3)])
    difference = jnp.where(live_rows[:, None], predicted - targets.astype(F32), 0.0)
    live_count = jnp.sum(lengths).astype(F32)
    squared = jnp.sum(difference * difference)
    grad_pred = difference.astype(BF)

    def pull_back(rows):
        return lax.dot_general(
            rows, projection, (((1,), (1,)), ((), ())), preferred_element_type=F32
        )

    arrived = swap(pull_back(grad_pred[2 * tok_rows :]).astype(BF), "dp", 1)
    pulled = pull_back(grad_pred[: 2 * tok_rows]) + arrived.astype(F32)
    pulled = pulled.reshape(2, tok_rows, 2 * width_half)
    half_rows = tok_rows // 2

    def own_half(array):
        return lax.dynamic_slice_in_dim(array, grp * width_half, width_half, array.ndim - 1)

    def other_half(array):
        return lax.dynamic_slice_in_dim(array, (1 - grp) * width_half, width_half, array.ndim - 1)

    first = pulled[:, :half_rows]
    second = pulled[:, half_rows:]
    first_in = swap(first[1].astype(BF), "dp", 2)
    second_in = swap(other_half(second).astype(BF), "grp", 1)
    first = first[0] + first_in.astype(F32)
    second = own_half(second) + second_in.astype(F32)
    first_in = swap(other_half(first).astype(BF), "grp", 1)
    second_in = swap(second[1].astype(BF), "dp", 2)
    grad_half = jnp.concatenate(
        [own_half(first) + first_in.astype(F32), second[0] + second_in.astype(F32)], axis=0
    )

    grad_proj_part = lax.dot_general(
        normed_all, grad_pred, (((0,), (0,)), ((), ())), preferred_element_type=F32
    ).astype(BF)
    grad_proj = line_scatter_sum(grad_proj_part, "mp", 1) / live_count

    gain_half = own_half(norm_gain)
    unit_half = own_half(hidden) * inverse_rms
    scaled = grad_half * gain_half
    inner_sum = jnp.sum(scaled * unit_half, axis=-1)
    tok_sums = jnp.concatenate([inner_sum, jnp.full((128,), squared, F32)])
    tok_sums = tok_sums + swap(tok_sums, "grp", 1)
    inner_sum = tok_sums[:tok_rows]
    mean_term = inner_sum[:, None] / D_S
    grad_hidden = inverse_rms * (scaled - unit_half * mean_term)

    sums = jnp.concatenate([jnp.sum(grad_half * unit_half, axis=0), tok_sums[tok_rows:]])
    for axis in ("dp", "mp"):
        flip = 1
        while flip < lax.axis_size(axis):
            sums = sums + swap(sums, axis, flip)
            flip *= 2
    grad_gain = sums[:width_half] / live_count
    distill_loss = sums[width_half] / (live_count * D_T)
    return (own_target[None], distill_loss, grad_proj, grad_gain, grad_hidden[None])


def solution(mesh):
    in_specs = (
        P("dp", None, "mp"),
        P("dp", None, None),
        P("dp", None, None),
        P("mp", None),
        P("dp", "mp", None),
        P("dp", "mp", None),
        P(),
        P(None, ("grp", "dp")),
        P(),
    )
    out_specs = (P("dp", "mp", "grp"), P(), P("mp", ("grp", "dp")), P("grp"), P("dp", "mp", "grp"))
    return jax.shard_map(body, mesh=mesh, in_specs=in_specs, out_specs=out_specs, check_vma=False)
```
